32 devices in a mesh: groups: 2 (over y), seq: 4 (over z), head: 2 (over x), rep: 2 (over core).
Axes of the slice: x: 2, y: 2, z: 4, core: 2. Of those that a mesh axis runs over, the one named last changes fastest.
Arguments:
- queries: bfloat16 [4, 512, 4096], P(('groups', 'head'), ('seq', 'rep')), parts along dimension 0, may hold values from -96 to 96
- keys: bfloat16 [4, 512, 4096], P(('groups', 'head'), ('seq', 'rep')), parts along dimension 0, may hold values from -4 to 4
- values: bfloat16 [4, 512, 4096], P(('groups', 'head'), ('seq', 'rep')), parts along dimension 0, may hold values from -6 to 6
- grad_out: bfloat16 [4, 512, 4096], P(('groups', 'head'), ('seq', 'rep')), parts along dimension 0, may hold values from -192 to 192
- gauge_key: bfloat16 [1024, 4096], P(('groups', 'head'), ('seq', 'rep')), parts along dimension 0, may hold values from -6 to 6
- gauge_value: bfloat16 [1024, 4096], P(('groups', 'head'), ('seq', 'rep')), parts along dimension 0, may hold values from -6 to 6
- block_keys: int32 [4, 4, 3], P(('groups', 'head')), parts along dimension 0, may hold values from 0 to 3, as said below
- block_count: int32 [4, 4], P(('groups', 'head')), parts along dimension 0, may hold values from 2 to 3, as said below
- gauge_block: int32 [4, 4], P(('groups', 'head')), parts along dimension 0, may hold values from 0 to 3
Outputs:
- grad_queries: bfloat16 [4, 512, 4096], P(('groups', 'head'), ('seq', 'rep')), parts along dimension 0
- grad_keys: bfloat16 [4, 512, 4096], P(('groups', 'head'), ('seq', 'rep')), parts along dimension 0
- grad_values: bfloat16 [4, 512, 4096], P(('groups', 'head'), ('seq', 'rep')), parts along dimension 0
- grad_gauge_key: float32 [1024, 4096], P(('groups', 'head'), ('seq', 'rep')), parts along dimension 0
- grad_gauge_value: float32 [1024, 4096], P(('groups', 'head'), ('seq', 'rep')), parts along dimension 0
The draws below stay inside these ranges and needn't reach their ends.
There are 2 independent parts, one for each index of `groups`. The reference program is written for one: setup_inputs(seed, part) draws one part's arguments, and reference() takes and returns one part's arrays. A program takes and returns all parts, laid end to end along the dimension named above; each array names one. Nothing has to cross between parts.
Inputs may be any that keep to these rules, and one draw needn't show every extreme that they name: `block_keys`: entry 0 of row [w, i] is i; the entries of a row are distinct. `block_count`: in every window some query block uses 3 key blocks.
All inputs are finite; a program needn't handle non-finite values.
Results may differ from the reference program's by a relative error of at most 0.005.
Values may be sent and summed in bfloat16 or wider, within the bound.
No kernel may reach another device: no remote copies, remote signals or barrier semaphores. Data moves between devices by JAX's collectives and lax.ppermute only.
A program may use at most 64 MiB of HBM per device.

```python
import math
import jax
import jax.numpy as jnp
from jax import lax

HEADS = 32
HD = 128
D = 4096
BLOCK = 128
K_MAX = 3
G = 512
WINDOWS = 2
LENGTH = 512
NBLK = 4
GB = 4


def draw_both(key):
    base = jax.random.fold_in(key, 7)
    key_raw = jnp.clip(jax.random.normal(jax.random.fold_in(base, 1), (WINDOWS, LENGTH, D), jnp.float32), -4.0, 4.0)
    query_raw = jnp.clip(jax.random.normal(jax.random.fold_in(base, 2), (WINDOWS, LENGTH, D), jnp.float32), -4.0, 4.0)
    queries = query_raw
    keys = key_raw
    return (queries, keys)


def draw_queries(key, part):
    return draw_both(key)[0].astype(jnp.bfloat16)


def draw_keys(key, part):
    return draw_both(key)[1].astype(jnp.bfloat16)


def draw_block_keys(key, part):
    block_total = LENGTH // BLOCK
    rows = jnp.arange(block_total)[:, None]
    cols = jnp.arange(block_total)[None, :]
    random_part = jax.random.randint(jax.random.fold_in(key, 11), (WINDOWS, block_total, block_total), 0, 1 << 20) * block_total
    ranked = random_part + cols[None, :, :]
    ranked = jnp.where((rows == cols)[None, :, :], 1 << 30, ranked)
    chosen = lax.top_k(ranked, K_MAX)[1]
    return chosen.astype(jnp.int32)


def draw_block_count(key, part):
    block_total = LENGTH // BLOCK
    counts = jax.random.randint(jax.random.fold_in(key, 21), (WINDOWS, block_total), 2, K_MAX + 1)
    picked = jax.random.randint(jax.random.fold_in(key, 22), (WINDOWS, 1), 0, block_total)
    counts = jnp.where(jnp.arange(block_total)[None, :] == picked, K_MAX, counts)
    return counts.astype(jnp.int32)


def with_ends(drawn, stream_key, smallest, top_value):
    extent = drawn.shape
    place = [jax.random.randint(jax.random.fold_in(stream_key, axis), (), 0, extent[axis]) for axis in range(len(extent))]
    drawn = drawn.at[tuple(place)].set(smallest)
    longest = extent.index(max(extent))
    place[longest] = (place[longest] + 1) % extent[longest]
    return drawn.at[tuple(place)].set(top_value)


def steps_of(rng, shape, shards, low, top_value):
    gain = 1.0
    for axis_at, parts in shards:
        heights = jax.random.uniform(jax.random.fold_in(jax.random.fold_in(rng, 6), axis_at), (parts,), jnp.float32, low / len(shards), top_value / len(shards))
        gain = gain * jnp.repeat(jnp.exp(heights), shape[axis_at] // parts).reshape((-1,) + (1,) * (len(shape) - 1 - axis_at))
    return gain


def normal_values(key, dims, deviation, reach, split=(), held_as=jnp.bfloat16):
    entries = jax.random.normal(key, dims, jnp.float32) * deviation
    if len(split) > 0:
        entries = steps_of(key, dims, split, -0.22, 0.18) * entries
    return jnp.clip(entries, min=-reach, max=reach).astype(held_as)


def setup_inputs(seed: int = 0, part: int = 0) -> dict:
    key_list = jax.random.split(jax.random.key(seed), 10)
    part_splits = jax.random.split(jax.random.fold_in(key_list[9], part), 10)
    return {
        "queries": draw_queries(jax.random.fold_in(jax.random.fold_in(key_list[9], part), 71), part),
        "keys": draw_keys(jax.random.fold_in(jax.random.fold_in(key_list[9], part), 71), part),
        "values": normal_values(part_splits[2], (WINDOWS, LENGTH, D), 1.0, 6.0, ((0, 2), (1, 8))),
        "grad_out": normal_values(part_splits[3], (WINDOWS, LENGTH, D), 32.0, 192.0, ((0, 2), (1, 8))),
        "gauge_key": normal_values(part_splits[4], (G, D), 1.0, 6.0, ((0, 2), (1, 8))),
        "gauge_value": normal_values(part_splits[5], (G, D), 1.0, 6.0, ((0, 2), (1, 8))),
        "block_keys": draw_block_keys(jax.random.fold_in(jax.random.fold_in(key_list[9], part), 71), part),
        "block_count": draw_block_count(jax.random.fold_in(jax.random.fold_in(key_list[9], part), 71), part),
        "gauge_block": with_ends(jax.random.randint(part_splits[8], (WINDOWS, NBLK), 0, GB), jax.random.fold_in(part_splits[8], 1), 0, GB - 1).astype(jnp.int32),
    }


def round_low(tensor):
    lowered = lax.optimization_barrier(tensor.astype(jnp.bfloat16))
    return lowered.astype(jnp.float32)

def window_grads(operands, gauge_keys, gauge_values):
    queries, keys, values, grad_out, key_lists, counts, chosen = operands
    block_total = LENGTH // BLOCK
    scaling = 1.0 / math.sqrt(HD)
    highest = lax.Precision.HIGHEST
    query_blocks = queries.astype(jnp.float32).reshape(block_total, BLOCK, HEADS, HD)
    grad_blocks = grad_out.astype(jnp.float32).reshape(block_total, BLOCK, HEADS, HD)
    key_blocks = keys.astype(jnp.float32).reshape(block_total, BLOCK, HEADS, HD)
    value_blocks = values.astype(jnp.float32).reshape(block_total, BLOCK, HEADS, HD)
    gauge_key_sel = gauge_keys.reshape(G // BLOCK, BLOCK, HEADS, HD)[chosen]
    gauge_value_sel = gauge_values.reshape(G // BLOCK, BLOCK, HEADS, HD)[chosen]
    key_slots = jnp.concatenate([key_blocks[key_lists].reshape(block_total, K_MAX * BLOCK, HEADS, HD), gauge_key_sel], axis=1)
    value_slots = jnp.concatenate([value_blocks[key_lists].reshape(block_total, K_MAX * BLOCK, HEADS, HD), gauge_value_sel], axis=1)
    scores = jnp.einsum('nqhd,nkhd->nhqk', query_blocks, key_slots, precision=highest) * scaling
    slot_block = jnp.arange((K_MAX + 1) * BLOCK, dtype=jnp.int32) // BLOCK
    allowed = (slot_block[None, :] < counts[:, None]) | (slot_block[None, :] == K_MAX)
    scores = jnp.where(allowed[:, None, None, :], scores, -jnp.inf)
    top_score = lax.optimization_barrier(jnp.max(scores, axis=-1, keepdims=True))
    weights = jnp.exp(scores - top_score)
    soft_weights = weights / lax.optimization_barrier(jnp.sum(weights, axis=-1, keepdims=True))
    grad_probs = jnp.einsum('nqhd,nkhd->nhqk', grad_blocks, value_slots, precision=highest)
    row_delta = lax.optimization_barrier(jnp.sum(soft_weights * grad_probs, axis=-1, keepdims=True))
    grad_scores = round_low(soft_weights * (grad_probs - row_delta) * scaling)
    probs_low = round_low(soft_weights)
    grad_query = jnp.einsum('nhqk,nkhd->nqhd', grad_scores, key_slots, precision=highest)
    grad_key_slots = jnp.einsum('nhqk,nqhd->nkhd', grad_scores, query_blocks, precision=highest)
    grad_value_slots = jnp.einsum('nhqk,nqhd->nkhd', probs_low, grad_blocks, precision=highest)
    listed = K_MAX * BLOCK
    block_hits = (key_lists[:, :, None] == jnp.arange(block_total, dtype=jnp.int32)[None, None, :]).astype(jnp.float32)
    gauge_hits = (chosen[:, None] == jnp.arange(G // BLOCK, dtype=jnp.int32)[None, :]).astype(jnp.float32)
    grad_key = jnp.einsum('nkj,nkbhd->jbhd', block_hits, grad_key_slots[:, :listed].reshape(block_total, K_MAX, BLOCK, HEADS, HD), precision=highest)
    grad_value = jnp.einsum('nkj,nkbhd->jbhd', block_hits, grad_value_slots[:, :listed].reshape(block_total, K_MAX, BLOCK, HEADS, HD), precision=highest)
    gauge_key_grad = jnp.einsum('ng,nbhd->gbhd', gauge_hits, grad_key_slots[:, listed:], precision=highest)
    gauge_value_grad = jnp.einsum('ng,nbhd->gbhd', gauge_hits, grad_value_slots[:, listed:], precision=highest)
    return (grad_query.reshape(LENGTH, D).astype(jnp.bfloat16), grad_key.reshape(LENGTH, D).astype(jnp.bfloat16), grad_value.reshape(LENGTH, D).astype(jnp.bfloat16), gauge_key_grad.reshape(G, D), gauge_value_grad.reshape(G, D))

def reference(queries, keys, values, grad_out, gauge_key, gauge_value, block_keys, block_count, gauge_block):
    gauge_keys = gauge_key.astype(jnp.float32)
    gauge_values = gauge_value.astype(jnp.float32)
    results = lax.map(partial_grads(gauge_keys, gauge_values), (queries, keys, values, grad_out, block_keys, block_count, gauge_block))
    grad_query, grad_key, grad_value, gauge_key_grad, gauge_value_grad = results
    return (grad_query, grad_key, grad_value, lax.optimization_barrier(jnp.sum(gauge_key_grad, axis=0)), lax.optimization_barrier(jnp.sum(gauge_value_grad, axis=0)))

def partial_grads(gauge_keys, gauge_values):

    def apply_window(operands):
        return window_grads(operands, gauge_keys, gauge_values)
    return apply_window
```

```python
import functools
import math

import jax
import jax.numpy as jnp
from jax import lax
from jax.experimental import pallas as pl
from jax.experimental.pallas import tpu as pltpu
from jax.sharding import PartitionSpec as P

HD = 128
BLOCK = 128
K_MAX = 3
TOKENS = ("seq", "rep")
ANY = pl.BlockSpec(memory_space=pl.ANY)
SMEM = pl.BlockSpec(memory_space=pltpu.SMEM)
VMEM_LIMIT = 48 * 1024 * 1024


def run_copies(copies):
    for copy in copies:
        copy.start()
    for copy in copies:
        copy.wait()


def pack_kernel(off, width, columns, order, place, *refs):
    arrays, gauges = refs[0:4], refs[4:6]
    sends, gauge_send = refs[6 : 6 + len(order)], refs[6 + len(order)]
    sems, gauge_sems = refs[-2:]
    me = place[0]
    copies = []
    for at, k in enumerate(order):
        start = pl.multiple_of((me ^ k) * columns + off, HD)
        for a in range(4):
            copies.append(
                pltpu.make_async_copy(
                    arrays[a].at[:, pl.ds(start, width)], sends[at].at[a], sems.at[at, a]
                )
            )
    for a in range(2):
        copies.append(
            pltpu.make_async_copy(
                gauges[a].at[:, pl.ds(off, width)], gauge_send.at[a], gauge_sems.at[a]
            )
        )
    run_copies(copies)


def grads_kernel(off, width, columns, order, gauge_order, place, lists, counts, chosen, *refs):
    n_tok, n_gauge = len(order), len(gauge_order)
    refs = list(refs)

    def take(count):
        out = refs[:count]
        del refs[:count]
        return out

    arrays, gauges = take(4), take(2)
    recvs, gauge_recvs = take(n_tok), take(n_gauge)
    outs, gauge_outs = take(n_tok + 1), take(n_gauge + 1)
    tok, gau, acc, gacc, res, in_sems, own_sems, gin_sems, gown_sems, out_sems, gout_sems = refs
    me, gauge_me = place[0], place[1]
    rows = arrays[0].shape[0]
    gauge_rows = gauges[0].shape[0]
    length = tok.shape[1]
    scaling = 1.0 / math.sqrt(HD)

    copies = []
    start = pl.multiple_of(me * columns + off, HD)
    for a in range(4):
        copies.append(
            pltpu.make_async_copy(
                arrays[a].at[:, pl.ds(start, width)],
                tok.at[a, pl.ds(pl.multiple_of(me * rows, rows), rows), :],
                own_sems.at[a],
            )
        )
    for at, k in enumerate(order):
        copies.append(
            pltpu.make_async_copy(
                recvs[at],
                tok.at[:, pl.ds(pl.multiple_of((me ^ k) * rows, rows), rows), :],
                in_sems.at[at],
            )
        )
    for a in range(2):
        copies.append(
            pltpu.make_async_copy(
                gauges[a].at[:, pl.ds(off, width)],
                gau.at[a, pl.ds(pl.multiple_of(gauge_me * gauge_rows, gauge_rows), gauge_rows), :],
                gown_sems.at[a],
            )
        )
    for at, k in enumerate(gauge_order):
        copies.append(
            pltpu.make_async_copy(
                gauge_recvs[at],
                gau.at[
                    :, pl.ds(pl.multiple_of((gauge_me ^ k) * gauge_rows, gauge_rows), gauge_rows), :
                ],
                gin_sems.at[at],
            )
        )
    for copy in copies:
        copy.start()
    acc[...] = jnp.zeros_like(acc)
    gacc[...] = jnp.zeros_like(gacc)
    for copy in copies:
        copy.wait()

    def block(n, carry):
        here = pl.ds(pl.multiple_of(n * BLOCK, BLOCK), BLOCK)
        slots = [
            pl.ds(pl.multiple_of(lists[n, j] * BLOCK, BLOCK), BLOCK) for j in range(K_MAX)
        ]
        gslot = pl.ds(pl.multiple_of(chosen[n] * BLOCK, BLOCK), BLOCK)
        row = lax.broadcasted_iota(jnp.int32, ((K_MAX + 1) * BLOCK, BLOCK), 0)
        allowed = (row < counts[n] * BLOCK) | (row >= K_MAX * BLOCK)
        for h in range(width // HD):
            lanes = slice(h * HD, (h + 1) * HD)
            q = tok[0, here, lanes]
            g = tok[3, here, lanes]
            k = jnp.concatenate([tok[1, s, lanes] for s in slots] + [gau[0, gslot, lanes]], axis=0)
            v = jnp.concatenate([tok[2, s, lanes] for s in slots] + [gau[1, gslot, lanes]], axis=0)
            last = (((1,), (1,)), ((), ()))
            scores = lax.dot_general(k, q, last, preferred_element_type=jnp.float32) * scaling
            scores = jnp.where(allowed, scores, -jnp.inf)
            weights = jnp.exp(scores - jnp.max(scores, axis=0, keepdims=True))
            inverse = 1.0 / jnp.sum(weights, axis=0, keepdims=True)
            probs = weights * inverse
            grad_probs = lax.dot_general(v, g, last, preferred_element_type=jnp.float32)
            delta = jnp.sum(probs * grad_probs, axis=0, keepdims=True)
            grad_scores = (probs * (grad_probs - delta) * scaling).astype(jnp.bfloat16)
            probs_low = probs.astype(jnp.bfloat16)
            res[0, here, lanes] = lax.dot_general(
                grad_scores, k, (((0,), (0,)), ((), ())), preferred_element_type=jnp.float32
            ).astype(jnp.bfloat16)
            dk = jnp.dot(grad_scores, q, preferred_element_type=jnp.float32)
            dv = jnp.dot(probs_low, g, preferred_element_type=jnp.float32)
            for j in range(K_MAX):
                part = slice(j * BLOCK, (j + 1) * BLOCK)
                acc[0, slots[j], lanes] += dk[part]
                acc[1, slots[j], lanes] += dv[part]
            gacc[0, gslot, lanes] += dk[K_MAX * BLOCK :]
            gacc[1, gslot, lanes] += dv[K_MAX * BLOCK :]
        return carry

    lax.fori_loop(0, length // BLOCK, block, 0)

    copies = []
    for at, k in enumerate((0,) + tuple(gauge_order)):
        copies.append(
            pltpu.make_async_copy(
                gacc.at[
                    :, pl.ds(pl.multiple_of((gauge_me ^ k) * gauge_rows, gauge_rows), gauge_rows), :
                ],
                gauge_outs[at],
                gout_sems.at[at],
            )
        )
    for copy in copies:
        copy.start()
    res[1] = acc[0].astype(jnp.bfloat16)
    res[2] = acc[1].astype(jnp.bfloat16)
    token_copies = []
    for at, k in enumerate((0,) + tuple(order)):
        token_copies.append(
            pltpu.make_async_copy(
                res.at[:, pl.ds(pl.multiple_of((me ^ k) * rows, rows), rows), :],
                outs[at],
                out_sems.at[at],
            )
        )
    run_copies(token_copies)
    for copy in copies:
        copy.wait()


def unpack_kernel(off, width, columns, order, held, place, *refs):
    parts = refs[held : held + len(order)]
    outs = refs[held + len(order) : held + len(order) + 3]
    sems = refs[-1]
    me = place[0]
    copies = []
    for at, k in enumerate(order):
        start = pl.multiple_of((me ^ k) * columns + off, HD)
        for a in range(3):
            copies.append(
                pltpu.make_async_copy(
                    parts[at].at[a], outs[a].at[:, pl.ds(start, width)], sems.at[at, a]
                )
            )
    run_copies(copies)


def chunks_of(heads):
    if heads == 1:
        return [(0, HD)]
    half = heads // 2
    return [(0, half * HD), (half * HD, (heads - half) * HD)]


def local(
    sizes,
    queries,
    keys,
    values,
    grad_out,
    gauge_key,
    gauge_value,
    block_keys,
    block_count,
    gauge_block,
):
    total, head_total = sizes
    rows, model = queries.shape[1], queries.shape[2]
    gauge_rows = gauge_key.shape[0]
    length, gauge_total = rows * total, gauge_rows * head_total
    columns = model // total
    bf16, f32 = jnp.bfloat16, jnp.float32
    arrays = [x[0] for x in (queries, keys, values, grad_out)]
    me = lax.axis_index(TOKENS).astype(jnp.int32)
    gauge_me = lax.axis_index("head").astype(jnp.int32)
    place = jnp.stack([me, gauge_me])
    order = tuple(range(total - 1, 0, -1))
    gauge_order = tuple(range(1, head_total))
    lists = (block_keys[0], block_count[0], gauge_block[0])
    params = pltpu.CompilerParams(vmem_limit_bytes=VMEM_LIMIT)

    def swap(x, axis, size, k):
        return lax.ppermute(x, axis, [(i, i ^ k) for i in range(size)])

    chunks = chunks_of(columns // HD)
    received = []
    for off, width in chunks:
        sends = pl.pallas_call(
            functools.partial(pack_kernel, off, width, columns, order),
            out_shape=[jax.ShapeDtypeStruct((4, rows, width), bf16)] * len(order)
            + [jax.ShapeDtypeStruct((2, gauge_rows, width), bf16)],
            in_specs=[SMEM] + [ANY] * 6,
            out_specs=[ANY] * (len(order) + 1),
            scratch_shapes=[
                pltpu.SemaphoreType.DMA((len(order), 4)),
                pltpu.SemaphoreType.DMA((2,)),
            ],
            name="pack",
        )(place, *arrays, gauge_key, gauge_value)
        gauge_send = sends[-1]
        recvs = [swap(s, TOKENS, total, k) for s, k in zip(sends, order)]
        gauge_recvs = [swap(gauge_send, "head", head_total, k) for k in gauge_order]
        received.append((recvs, gauge_recvs))

    outs = None
    gauge_parts = []
    returned = []
    for (off, width), (recvs, gauge_recvs) in zip(chunks, received):
        pieces = pl.pallas_call(
            functools.partial(grads_kernel, off, width, columns, order, gauge_order),
            out_shape=[jax.ShapeDtypeStruct((3, rows, width), bf16)] * total
            + [jax.ShapeDtypeStruct((2, gauge_rows, width), f32)] * head_total,
            in_specs=[SMEM] * 4 + [ANY] * (6 + len(order) + len(gauge_order)),
            out_specs=[ANY] * (total + head_total),
            scratch_shapes=[
                pltpu.VMEM((4, length, width), bf16),
                pltpu.VMEM((2, gauge_total, width), bf16),
                pltpu.VMEM((2, length, width), f32),
                pltpu.VMEM((2, gauge_total, width), f32),
                pltpu.VMEM((3, length, width), bf16),
                pltpu.SemaphoreType.DMA((max(len(order), 1),)),
                pltpu.SemaphoreType.DMA((4,)),
                pltpu.SemaphoreType.DMA((max(len(gauge_order), 1),)),
                pltpu.SemaphoreType.DMA((2,)),
                pltpu.SemaphoreType.DMA((total,)),
                pltpu.SemaphoreType.DMA((head_total,)),
            ],
            compiler_params=params,
            name="grads",
        )(place, *lists, *arrays, gauge_key, gauge_value, *recvs, *gauge_recvs)
        back = [pieces[0]] + [swap(p, TOKENS, total, k) for p, k in zip(pieces[1:total], order)]
        gauge_back = [
            swap(p, "head", head_total, k) for p, k in zip(pieces[total + 1 :], gauge_order)
        ]
        gauge_parts.append(functools.reduce(jnp.add, gauge_back, pieces[total]))
        returned.append(back)

    for (off, width), back in zip(chunks, returned):
        held = 0 if outs is None else 3
        slots = (0,) + order
        outs = pl.pallas_call(
            functools.partial(unpack_kernel, off, width, columns, slots, held),
            out_shape=[jax.ShapeDtypeStruct((rows, model), bf16)] * 3,
            in_specs=[SMEM] + [ANY] * (held + total),
            out_specs=[ANY] * 3,
            scratch_shapes=[pltpu.SemaphoreType.DMA((total, 3))],
            input_output_aliases={1 + a: a for a in range(held)},
            name="unpack",
        )(place, *(outs if held else []), *back)

    gauge_grads = jnp.concatenate(gauge_parts, axis=2)
    return (outs[0][None], outs[1][None], outs[2][None], gauge_grads[0], gauge_grads[1])


def solution(mesh):
    tokens = P(("groups", "head"), TOKENS, None)
    gauges = P(("groups", "head"), TOKENS)
    lists = P(("groups", "head"), None, None)
    counts = P(("groups", "head"), None)
    sizes = (mesh.shape["seq"] * mesh.shape["rep"], mesh.shape["head"])
    return jax.shard_map(
        functools.partial(local, sizes),
        mesh=mesh,
        in_specs=(tokens,) * 4 + (gauges,) * 2 + (lists, counts, counts),
        out_specs=(tokens,) * 3 + (gauges,) * 2,
        check_vma=False,
    )
```

```python
import functools
import math

import jax
import jax.numpy as jnp
from jax import lax
from jax.experimental import pallas as pl
from jax.experimental.pallas import tpu as pltpu
from jax.sharding import PartitionSpec as P

HD = 128
BLOCK = 128
K_MAX = 3
EARLY = 5
TOKENS = ("seq", "rep")
ANY = pl.BlockSpec(memory_space=pl.ANY)
SMEM = pl.BlockSpec(memory_space=pltpu.SMEM)
VMEM_LIMIT = 16 * 1024 * 1024


def run_copies(copies):
    for copy in copies:
        copy.start()
    for copy in copies:
        copy.wait()


def pack_kernel(off, width, columns, order, waits, with_gauges, place, *refs):
    arrays, gauges = refs[0:4], refs[4:6]
    sends = refs[6 + waits : 6 + waits + len(order)]
    sems, gauge_sems = refs[-2:]
    me = place[0]
    copies = []
    for at, k in enumerate(order):
        start = pl.multiple_of((me ^ k) * columns + off, HD)
        for a in range(4):
            copies.append(
                pltpu.make_async_copy(
                    arrays[a].at[:, pl.ds(start, width)], sends[at].at[a], sems.at[at, a]
                )
            )
    if with_gauges:
        for a in range(2):
            copies.append(pltpu.make_async_copy(gauges[a], refs[-3].at[a], gauge_sems.at[a]))
    run_copies(copies)


def grads_kernel(
    off, width, columns, order, gauge_order, waits, place, lists, counts, chosen, *refs
):
    n_tok, n_gauge = len(order), len(gauge_order)
    refs = list(refs)

    def take(count):
        out = refs[:count]
        del refs[:count]
        return out

    arrays, gauges = take(4), take(2)
    recvs, gauge_recvs = take(n_tok), take(n_gauge)
    take(waits)
    outs, gauge_outs = take(n_tok + 1), take(n_gauge + 1)
    tok, gau, acc, gacc, res, in_sems, own_sems, gin_sems, gown_sems, out_sems, gout_sems = refs
    me, gauge_me = place[0], place[1]
    rows = arrays[0].shape[0]
    gauge_rows = gauges[0].shape[0]
    length = tok.shape[1]
    scaling = 1.0 / math.sqrt(HD)

    copies = []
    start = pl.multiple_of(me * columns + off, HD)
    for a in range(4):
        copies.append(
            pltpu.make_async_copy(
                arrays[a].at[:, pl.ds(start, width)],
                tok.at[a, pl.ds(pl.multiple_of(me * rows, rows), rows), :],
                own_sems.at[a],
            )
        )
    for at, k in enumerate(order):
        copies.append(
            pltpu.make_async_copy(
                recvs[at],
                tok.at[:, pl.ds(pl.multiple_of((me ^ k) * rows, rows), rows), :],
                in_sems.at[at],
            )
        )
    for a in range(2):
        copies.append(
            pltpu.make_async_copy(
                gauges[a].at[:, pl.ds(off, width)],
                gau.at[a, pl.ds(pl.multiple_of(gauge_me * gauge_rows, gauge_rows), gauge_rows), :],
                gown_sems.at[a],
            )
        )
    for at, k in enumerate(gauge_order):
        copies.append(
            pltpu.make_async_copy(
                gauge_recvs[at].at[:, :, pl.ds(off, width)],
                gau.at[
                    :, pl.ds(pl.multiple_of((gauge_me ^ k) * gauge_rows, gauge_rows), gauge_rows), :
                ],
                gin_sems.at[at],
            )
        )
    for copy in copies:
        copy.start()
    acc[...] = jnp.zeros_like(acc)
    gacc[...] = jnp.zeros_like(gacc)
    for copy in copies:
        copy.wait()

    def block(n, carry):
        here = pl.ds(pl.multiple_of(n * BLOCK, BLOCK), BLOCK)
        slots = [
            pl.ds(pl.multiple_of(lists[n, j] * BLOCK, BLOCK), BLOCK) for j in range(K_MAX)
        ]
        gslot = pl.ds(pl.multiple_of(chosen[n] * BLOCK, BLOCK), BLOCK)
        row = lax.broadcasted_iota(jnp.int32, ((K_MAX + 1) * BLOCK, BLOCK), 0)
        allowed = (row < counts[n] * BLOCK) | (row >= K_MAX * BLOCK)
        for h in range(width // HD):
            lanes = slice(h * HD, (h + 1) * HD)
            q = tok[0, here, lanes]
            g = tok[3, here, lanes]
            k = jnp.concatenate([tok[1, s, lanes] for s in slots] + [gau[0, gslot, lanes]], axis=0)
            v = jnp.concatenate([tok[2, s, lanes] for s in slots] + [gau[1, gslot, lanes]], axis=0)
            last = (((1,), (1,)), ((), ()))
            scores = lax.dot_general(k, q, last, preferred_element_type=jnp.float32) * scaling
            scores = jnp.where(allowed, scores, -jnp.inf)
            weights = jnp.exp(scores - jnp.max(scores, axis=0, keepdims=True))
            inverse = 1.0 / jnp.sum(weights, axis=0, keepdims=True)
            probs = weights * inverse
            grad_probs = lax.dot_general(v, g, last, preferred_element_type=jnp.float32)
            delta = jnp.sum(probs * grad_probs, axis=0, keepdims=True)
            grad_scores = (probs * (grad_probs - delta) * scaling).astype(jnp.bfloat16)
            probs_low = probs.astype(jnp.bfloat16)
            res[0, here, lanes] = lax.dot_general(
                grad_scores, k, (((0,), (0,)), ((), ())), preferred_element_type=jnp.float32
            ).astype(jnp.bfloat16)
            dk = jnp.dot(grad_scores, q, preferred_element_type=jnp.float32)
            dv = jnp.dot(probs_low, g, preferred_element_type=jnp.float32)
            for j in range(K_MAX):
                part = slice(j * BLOCK, (j + 1) * BLOCK)
                acc[0, slots[j], lanes] += dk[part]
                acc[1, slots[j], lanes] += dv[part]
            gacc[0, gslot, lanes] += dk[K_MAX * BLOCK :]
            gacc[1, gslot, lanes] += dv[K_MAX * BLOCK :]
        return carry

    lax.fori_loop(0, length // BLOCK, block, 0)

    copies = []
    for at, k in enumerate((0,) + tuple(gauge_order)):
        copies.append(
            pltpu.make_async_copy(
                gacc.at[
                    :, pl.ds(pl.multiple_of((gauge_me ^ k) * gauge_rows, gauge_rows), gauge_rows), :
                ],
                gauge_outs[at],
                gout_sems.at[at],
            )
        )
    for copy in copies:
        copy.start()
    res[1] = acc[0].astype(jnp.bfloat16)
    res[2] = acc[1].astype(jnp.bfloat16)
    token_copies = []
    for at, k in enumerate((0,) + tuple(order)):
        token_copies.append(
            pltpu.make_async_copy(
                res.at[:, pl.ds(pl.multiple_of((me ^ k) * rows, rows), rows), :],
                outs[at],
                out_sems.at[at],
            )
        )
    run_copies(token_copies)
    for copy in copies:
        copy.wait()


def unpack_kernel(off, width, columns, order, held, place, *refs):
    parts = refs[held : held + len(order)]
    outs = refs[held + len(order) : held + len(order) + 3]
    sems = refs[-1]
    me = place[0]
    copies = []
    for at, k in enumerate(order):
        start = pl.multiple_of((me ^ k) * columns + off, HD)
        for a in range(3):
            copies.append(
                pltpu.make_async_copy(
                    parts[at].at[a], outs[a].at[:, pl.ds(start, width)], sems.at[at, a]
                )
            )
    run_copies(copies)


def chunks_of(heads):
    if heads == 1:
        return [(0, HD)]
    half = heads // 2
    return [(0, half * HD), (half * HD, (heads - half) * HD)]


def local(
    sizes,
    queries,
    keys,
    values,
    grad_out,
    gauge_key,
    gauge_value,
    block_keys,
    block_count,
    gauge_block,
):
    total, head_total = sizes
    rows, model = queries.shape[1], queries.shape[2]
    gauge_rows = gauge_key.shape[0]
    length, gauge_total = rows * total, gauge_rows * head_total
    columns = model // total
    bf16, f32 = jnp.bfloat16, jnp.float32
    arrays = [x[0] for x in (queries, keys, values, grad_out)]
    arrays = [pltpu.with_memory_space_constraint(x, pltpu.HBM) for x in arrays]
    gauge_key, gauge_value = [
        pltpu.with_memory_space_constraint(x, pltpu.HBM) for x in (gauge_key, gauge_value)
    ]
    me = lax.axis_index(TOKENS).astype(jnp.int32)
    gauge_me = lax.axis_index("head").astype(jnp.int32)
    place = jnp.stack([me, gauge_me])
    half = total // 2
    order = tuple(k for i in range(half) for k in (total - 1 - i, half - 1 - i) if k)
    gauge_order = tuple(range(1, head_total))
    lists = (block_keys[0], block_count[0], gauge_block[0])
    params = pltpu.CompilerParams(vmem_limit_bytes=VMEM_LIMIT)

    def swap(x, axis, size, k):
        return lax.ppermute(x, axis, [(i, i ^ k) for i in range(size)])

    chunks = chunks_of(columns // HD)

    def pack(chunk, part, after, with_gauges):
        off, width = chunk
        shapes = [jax.ShapeDtypeStruct((4, rows, width), bf16)] * len(part)
        if with_gauges:
            shapes.append(jax.ShapeDtypeStruct((2, gauge_rows, columns), bf16))
        return pl.pallas_call(
            functools.partial(
                pack_kernel, off, width, columns, part, len(after), with_gauges
            ),
            out_shape=shapes,
            in_specs=[SMEM] + [ANY] * (6 + len(after)),
            out_specs=[ANY] * len(shapes),
            scratch_shapes=[
                pltpu.SemaphoreType.DMA((len(part), 4)),
                pltpu.SemaphoreType.DMA((2,)),
            ],
            compiler_params=params,
            name="pack",
        )(place, *arrays, gauge_key, gauge_value, *after)

    def grads(chunk, recvs, after):
        off, width = chunk
        return pl.pallas_call(
            functools.partial(
                grads_kernel, off, width, columns, order, gauge_order, len(after)
            ),
            out_shape=[jax.ShapeDtypeStruct((3, rows, width), bf16)] * total
            + [jax.ShapeDtypeStruct((2, gauge_rows, width), f32)] * head_total,
            in_specs=[SMEM] * 4 + [ANY] * (6 + len(order) + len(gauge_order) + len(after)),
            out_specs=[ANY] * (total + head_total),
            scratch_shapes=[
                pltpu.VMEM((4, length, width), bf16),
                pltpu.VMEM((2, gauge_total, width), bf16),
                pltpu.VMEM((2, length, width), f32),
                pltpu.VMEM((2, gauge_total, width), f32),
                pltpu.VMEM((3, length, width), bf16),
                pltpu.SemaphoreType.DMA((max(len(order), 1),)),
                pltpu.SemaphoreType.DMA((4,)),
                pltpu.SemaphoreType.DMA((max(len(gauge_order), 1),)),
                pltpu.SemaphoreType.DMA((2,)),
                pltpu.SemaphoreType.DMA((total,)),
                pltpu.SemaphoreType.DMA((head_total,)),
            ],
            compiler_params=params,
            cost_estimate=pl.CostEstimate(
                flops=10 * (K_MAX + 1) * BLOCK * length * width * 16,
                bytes_accessed=14 * length * width,
                transcendentals=0,
            ),
            name="grads",
        )(place, *lists, *arrays, gauge_key, gauge_value, *recvs, *gauge_recvs, *after)

    def give_back(pieces):
        gauge_back = [
            swap(p, "head", head_total, k) for p, k in zip(pieces[total + 1 :], gauge_order)
        ]
        back = [pieces[0]] + [swap(p, TOKENS, total, k) for p, k in zip(pieces[1:total], order)]
        return back, functools.reduce(jnp.add, gauge_back, pieces[total])

    def send(packed, part):
        return [swap(s, TOKENS, total, k) for s, k in zip(packed, part)]

    *packed, gauge_send = pack(chunks[0], order, [], True)
    gauge_recvs = [swap(gauge_send, "head", head_total, k) for k in gauge_order]
    recvs = send(packed, order)
    returned, gauge_parts = [], []
    for at, chunk in enumerate(chunks):
        after = [returned[-1][0][1]] if returned else []
        ahead = []
        if at + 1 < len(chunks):
            ahead = send(pack(chunks[at + 1], order[:EARLY], recvs[:1], False), order[:EARLY])
        pieces = grads(chunk, recvs, after)
        if at + 1 < len(chunks):
            late = pack(chunks[at + 1], order[EARLY:], pieces[:1], False)
            recvs = ahead + send(late, order[EARLY:])
        returned.append(give_back(pieces))
    gauge_parts = [part for _, part in returned]
    returned = [back for back, _ in returned]
    outs = None

    for (off, width), back in zip(chunks, returned):
        held = 0 if outs is None else 3
        slots = (0,) + order
        outs = pl.pallas_call(
            functools.partial(unpack_kernel, off, width, columns, slots, held),
            out_shape=[jax.ShapeDtypeStruct((rows, model), bf16)] * 3,
            in_specs=[SMEM] + [ANY] * (held + total),
            out_specs=[ANY] * 3,
            scratch_shapes=[pltpu.SemaphoreType.DMA((total, 3))],
            input_output_aliases={1 + a: a for a in range(held)},
            compiler_params=params,
            name="unpack",
        )(place, *(outs if held else []), *back)

    gauge_grads = jnp.concatenate(gauge_parts, axis=2)
    return (outs[0][None], outs[1][None], outs[2][None], gauge_grads[0], gauge_grads[1])


def solution(mesh):
    tokens = P(("groups", "head"), TOKENS, None)
    gauges = P(("groups", "head"), TOKENS)
    lists = P(("groups", "head"), None, None)
    counts = P(("groups", "head"), None)
    sizes = (mesh.shape["seq"] * mesh.shape["rep"], mesh.shape["head"])
    return jax.shard_map(
        functools.partial(local, sizes),
        mesh=mesh,
        in_specs=(tokens,) * 4 + (gauges,) * 2 + (lists, counts, counts),
        out_specs=(tokens,) * 3 + (gauges,) * 2,
        check_vma=False,
    )
```

```python
import functools
import math

import jax
import jax.numpy as jnp
from jax import lax
from jax.experimental import pallas as pl
from jax.experimental.pallas import tpu as pltpu
from jax.sharding import PartitionSpec as P

HD = 128
BLOCK = 128
K_MAX = 3
AHEAD = 0
TOKENS = ("seq", "rep")
ANY = pl.BlockSpec(memory_space=pl.ANY)
SMEM = pl.BlockSpec(memory_space=pltpu.SMEM)
VMEM_LIMIT = 16 * 1024 * 1024


def run_copies(copies):
    for copy in copies:
        copy.start()
    for copy in copies:
        copy.wait()


def pack_kernel(off, width, columns, order, waits, with_gauges, place, *refs):
    arrays, gauges = refs[0:4], refs[4:6]
    sends = refs[6 + waits : 6 + waits + len(order)]
    sems, gauge_sems = refs[-2:]
    me = place[0]
    copies = []
    for at, k in enumerate(order):
        start = pl.multiple_of((me ^ k) * columns + off, HD)
        for a in range(4):
            copies.append(
                pltpu.make_async_copy(
                    arrays[a].at[:, pl.ds(start, width)], sends[at].at[a], sems.at[at, a]
                )
            )
    if with_gauges:
        for a in range(2):
            copies.append(pltpu.make_async_copy(gauges[a], refs[-3].at[a], gauge_sems.at[a]))
    run_copies(copies)


def grads_kernel(
    off, width, columns, order, gauge_order, waits, held, place, lists, counts, chosen, *refs
):
    n_tok, n_gauge = len(order), len(gauge_order)
    refs = list(refs)

    def take(count):
        out = refs[:count]
        del refs[:count]
        return out

    arrays, gauges = take(4), take(2)
    recvs, gauge_recvs = take(n_tok), take(n_gauge)
    take(waits + held)
    outs, gauge_outs = take(n_tok + 1), take(n_gauge + 1)
    tok, gau, acc, gacc, res, in_sems, own_sems, gin_sems, gown_sems, out_sems, gout_sems = refs
    me, gauge_me = place[0], place[1]
    rows = arrays[0].shape[0]
    gauge_rows = gauges[0].shape[0]
    length = tok.shape[1]
    scaling = 1.0 / math.sqrt(HD)

    copies = []
    start = pl.multiple_of(me * columns + off, HD)
    for a in range(4):
        copies.append(
            pltpu.make_async_copy(
                arrays[a].at[:, pl.ds(start, width)],
                tok.at[a, pl.ds(pl.multiple_of(me * rows, rows), rows), :],
                own_sems.at[a],
            )
        )
    for at, k in enumerate(order):
        copies.append(
            pltpu.make_async_copy(
                recvs[at],
                tok.at[:, pl.ds(pl.multiple_of((me ^ k) * rows, rows), rows), :],
                in_sems.at[at],
            )
        )
    for a in range(2):
        copies.append(
            pltpu.make_async_copy(
                gauges[a].at[:, pl.ds(off, width)],
                gau.at[a, pl.ds(pl.multiple_of(gauge_me * gauge_rows, gauge_rows), gauge_rows), :],
                gown_sems.at[a],
            )
        )
    for at, k in enumerate(gauge_order):
        copies.append(
            pltpu.make_async_copy(
                gauge_recvs[at].at[:, :, pl.ds(off, width)],
                gau.at[
                    :, pl.ds(pl.multiple_of((gauge_me ^ k) * gauge_rows, gauge_rows), gauge_rows), :
                ],
                gin_sems.at[at],
            )
        )
    for copy in copies:
        copy.start()
    acc[...] = jnp.zeros_like(acc)
    gacc[...] = jnp.zeros_like(gacc)
    for copy in copies:
        copy.wait()

    def block(n, carry):
        here = pl.ds(pl.multiple_of(n * BLOCK, BLOCK), BLOCK)
        slots = [
            pl.ds(pl.multiple_of(lists[n, j] * BLOCK, BLOCK), BLOCK) for j in range(K_MAX)
        ]
        gslot = pl.ds(pl.multiple_of(chosen[n] * BLOCK, BLOCK), BLOCK)
        third = jnp.where(counts[n] == K_MAX, 0.0, -jnp.inf).astype(jnp.float32)
        base, listed = (K_MAX - 1) * BLOCK, K_MAX * BLOCK
        for h in range(width // HD):
            lanes = slice(h * HD, (h + 1) * HD)
            q = tok[0, here, lanes]
            g = tok[3, here, lanes]
            k = jnp.concatenate([tok[1, s, lanes] for s in slots] + [gau[0, gslot, lanes]], axis=0)
            v = jnp.concatenate([tok[2, s, lanes] for s in slots] + [gau[1, gslot, lanes]], axis=0)
            last = (((1,), (1,)), ((), ()))
            scores = lax.dot_general(k, q, last, preferred_element_type=jnp.float32)
            grad_probs = lax.dot_general(v, g, last, preferred_element_type=jnp.float32)
            scores = jnp.concatenate(
                [scores[:base], scores[base:listed] + third, scores[listed:]], axis=0
            )
            top = jnp.max(scores, axis=0, keepdims=True)
            weights = jnp.exp2((scores - top) * (scaling * math.log2(math.e)))
            inverse = 1.0 / jnp.sum(weights, axis=0, keepdims=True)
            delta = jnp.sum(weights * grad_probs, axis=0, keepdims=True) * inverse
            probs = weights * inverse
            grad_scores = (probs * ((grad_probs - delta) * scaling)).astype(jnp.bfloat16)
            probs_low = probs.astype(jnp.bfloat16)
            dk = jnp.dot(grad_scores, q, preferred_element_type=jnp.float32)
            dv = jnp.dot(probs_low, g, preferred_element_type=jnp.float32)
            res[0, here, lanes] = lax.dot_general(
                grad_scores, k, (((0,), (0,)), ((), ())), preferred_element_type=jnp.float32
            ).astype(jnp.bfloat16)
            for j in range(K_MAX):
                part = slice(j * BLOCK, (j + 1) * BLOCK)
                acc[0, slots[j], lanes] += dk[part]
                acc[1, slots[j], lanes] += dv[part]
            gacc[0, gslot, lanes] += dk[listed:]
            gacc[1, gslot, lanes] += dv[listed:]
        return carry

    lax.fori_loop(0, length // BLOCK, block, 0, unroll=4)

    copies = []
    for at, k in enumerate((0,) + tuple(gauge_order)):
        copies.append(
            pltpu.make_async_copy(
                gacc.at[
                    :, pl.ds(pl.multiple_of((gauge_me ^ k) * gauge_rows, gauge_rows), gauge_rows), :
                ],
                gauge_outs[at],
                gout_sems.at[at],
            )
        )
    for copy in copies:
        copy.start()
    res[1] = acc[0].astype(jnp.bfloat16)
    res[2] = acc[1].astype(jnp.bfloat16)
    token_copies = []
    for k in range(n_tok + 1):
        token_copies.append(
            pltpu.make_async_copy(
                res.at[:, pl.ds(pl.multiple_of((me ^ k) * rows, rows), rows), :],
                outs[k].at[:, :, pl.ds(off, width)],
                out_sems.at[k],
            )
        )
    run_copies(token_copies)
    for copy in copies:
        copy.wait()


def unpack_kernel(columns, order, place, *refs):
    outs, sems = refs[-4:-1], refs[-1]
    me = place[0]
    copies = []
    for at, k in enumerate(order):
        start = pl.multiple_of((me ^ k) * columns, HD)
        for a in range(3):
            copies.append(
                pltpu.make_async_copy(
                    refs[at].at[a], outs[a].at[:, pl.ds(start, columns)], sems.at[at, a]
                )
            )
    run_copies(copies)


def chunks_of(heads):
    if heads == 1:
        return [(0, HD)]
    half = heads // 2
    return [(0, half * HD), (half * HD, (heads - half) * HD)]


def local(
    sizes,
    queries,
    keys,
    values,
    grad_out,
    gauge_key,
    gauge_value,
    block_keys,
    block_count,
    gauge_block,
):
    total, head_total = sizes
    rows, model = queries.shape[1], queries.shape[2]
    gauge_rows = gauge_key.shape[0]
    length, gauge_total = rows * total, gauge_rows * head_total
    columns = model // total
    bf16, f32 = jnp.bfloat16, jnp.float32
    arrays = [x[0] for x in (queries, keys, values, grad_out)]
    arrays = [pltpu.with_memory_space_constraint(x, pltpu.HBM) for x in arrays]
    gauge_key, gauge_value = [
        pltpu.with_memory_space_constraint(x, pltpu.HBM) for x in (gauge_key, gauge_value)
    ]
    me = lax.axis_index(TOKENS).astype(jnp.int32)
    gauge_me = lax.axis_index("head").astype(jnp.int32)
    place = jnp.stack([me, gauge_me])
    half = total // 2
    order = tuple(k for i in range(half) for k in (total - 1 - i, half - 1 - i) if k)
    gauge_order = tuple(range(1, head_total))
    lists = (block_keys[0], block_count[0], gauge_block[0])
    params = pltpu.CompilerParams(vmem_limit_bytes=VMEM_LIMIT)

    def swap(x, axis, size, k):
        return lax.ppermute(x, axis, [(i, i ^ k) for i in range(size)])

    chunks = chunks_of(columns // HD)

    def pack(chunk, part, after, with_gauges):
        off, width = chunk
        shapes = [jax.ShapeDtypeStruct((4, rows, width), bf16)] * len(part)
        if with_gauges:
            shapes.append(jax.ShapeDtypeStruct((2, gauge_rows, columns), bf16))
        return pl.pallas_call(
            functools.partial(
                pack_kernel, off, width, columns, part, len(after), with_gauges
            ),
            out_shape=shapes,
            in_specs=[SMEM] + [ANY] * (6 + len(after)),
            out_specs=[ANY] * len(shapes),
            scratch_shapes=[
                pltpu.SemaphoreType.DMA((len(part), 4)),
                pltpu.SemaphoreType.DMA((2,)),
            ],
            compiler_params=params,
            name="pack",
        )(place, *arrays, gauge_key, gauge_value, *after)

    def grads(chunk, recvs, order, after, held):
        off, width = chunk
        return pl.pallas_call(
            functools.partial(
                grads_kernel, off, width, columns, order, gauge_order, len(after), len(held)
            ),
            out_shape=[jax.ShapeDtypeStruct((3, rows, columns), bf16)] * total
            + [jax.ShapeDtypeStruct((2, gauge_rows, width), f32)] * head_total,
            in_specs=[SMEM] * 4
            + [ANY] * (6 + len(order) + len(gauge_order) + len(after) + len(held)),
            out_specs=[ANY] * (total + head_total),
            scratch_shapes=[
                pltpu.VMEM((4, length, width), bf16),
                pltpu.VMEM((2, gauge_total, width), bf16),
                pltpu.VMEM((2, length, width), f32),
                pltpu.VMEM((2, gauge_total, width), f32),
                pltpu.VMEM((3, length, width), bf16),
                pltpu.SemaphoreType.DMA((max(len(order), 1),)),
                pltpu.SemaphoreType.DMA((4,)),
                pltpu.SemaphoreType.DMA((max(len(gauge_order), 1),)),
                pltpu.SemaphoreType.DMA((2,)),
                pltpu.SemaphoreType.DMA((total,)),
                pltpu.SemaphoreType.DMA((head_total,)),
            ],
            compiler_params=params,
            cost_estimate=pl.CostEstimate(
                flops=10 * (K_MAX + 1) * BLOCK * length * width * 16,
                bytes_accessed=14 * length * width,
                transcendentals=0,
            ),
            input_output_aliases={
                10 + len(order) + len(gauge_order) + len(after) + i: i for i in range(len(held))
            },
            name="grads",
        )(place, *lists, *arrays, gauge_key, gauge_value, *recvs, *gauge_recvs, *after, *held)

    def send(packed, part):
        return [swap(s, TOKENS, total, k) for s, k in zip(packed, part)]

    *packed, gauge_send = pack(chunks[0], order, [], True)
    gauge_recvs = [swap(gauge_send, "head", head_total, k) for k in gauge_order]
    recvs = send(packed, order)
    pieces, gauge_sums = [], []
    for at, chunk in enumerate(chunks):
        ahead = []
        if at + 1 < len(chunks):
            ahead = send(pack(chunks[at + 1], order, recvs[:1], False), order)
        out = grads(chunk, recvs, order, ahead[:AHEAD], pieces)
        pieces = out[:total]
        gauge_back = [
            swap(x, "head", head_total, k) for x, k in zip(out[total + 1 :], gauge_order)
        ]
        gauge_sums.append(functools.reduce(jnp.add, gauge_back, out[total]))
        recvs = ahead
    back = [pieces[0]] + [swap(pieces[k], TOKENS, total, k) for k in order]
    gauge_sum = jnp.concatenate(gauge_sums, axis=2)
    gauge_grads = [gauge_sum[0], gauge_sum[1]]
    outs = pl.pallas_call(
        functools.partial(unpack_kernel, columns, (0, *order)),
        out_shape=[jax.ShapeDtypeStruct((rows, model), bf16)] * 3,
        in_specs=[SMEM] + [ANY] * (total + 2),
        out_specs=[ANY] * 3,
        scratch_shapes=[pltpu.SemaphoreType.DMA((total, 3))],
        compiler_params=params,
        name="unpack",
    )(place, *back, *gauge_grads)
    return (outs[0][None], outs[1][None], outs[2][None], *gauge_grads)


def solution(mesh):
    tokens = P(("groups", "head"), TOKENS, None)
    gauges = P(("groups", "head"), TOKENS)
    lists = P(("groups", "head"), None, None)
    counts = P(("groups", "head"), None)
    sizes = (mesh.shape["seq"] * mesh.shape["rep"], mesh.shape["head"])
    return jax.shard_map(
        functools.partial(local, sizes),
        mesh=mesh,
        in_specs=(tokens,) * 4 + (gauges,) * 2 + (lists, counts, counts),
        out_specs=(tokens,) * 3 + (gauges,) * 2,
        check_vma=False,
    )
```

```python
import functools
import math

import jax
import jax.numpy as jnp
from jax import lax
from jax.experimental import pallas as pl
from jax.experimental.pallas import tpu as pltpu
from jax.sharding import PartitionSpec as P

HD = 128
BLOCK = 128
K_MAX = 3
EARLY = 2
EHOLD = 5
TAIL = 3
TOKENS = ("seq", "rep")
ANY = pl.BlockSpec(memory_space=pl.ANY)
SMEM = pl.BlockSpec(memory_space=pltpu.SMEM)
VMEM_LIMIT = 16 * 1024 * 1024


def run_copies(copies):
    for copy in copies:
        copy.start()
    for copy in copies:
        copy.wait()


def pack_kernel(off, width, columns, order, waits, with_gauges, place, *refs):
    arrays, gauges = refs[0:4], refs[4:6]
    sends = refs[6 + waits : 6 + waits + len(order)]
    sems, gauge_sems = refs[-2:]
    me = place[0]
    copies = []
    for at, k in enumerate(order):
        start = pl.multiple_of((me ^ k) * columns + off, HD)
        for a in range(4):
            copies.append(
                pltpu.make_async_copy(
                    arrays[a].at[:, pl.ds(start, width)], sends[at].at[a], sems.at[at, a]
                )
            )
    if with_gauges:
        for a in range(2):
            copies.append(pltpu.make_async_copy(gauges[a], refs[-3].at[a], gauge_sems.at[a]))
    run_copies(copies)


def grads_kernel(
    off, width, columns, order, targets, gauge_order, waits, held, place, lists, counts, chosen, *refs
):
    n_tok, n_gauge = len(order), len(gauge_order)
    refs = list(refs)

    def take(count):
        out = refs[:count]
        del refs[:count]
        return out

    arrays, gauges = take(4), take(2)
    recvs, gauge_recvs = take(n_tok), take(n_gauge)
    take(waits + held)
    outs, gauge_outs = take(n_tok + 1), take(n_gauge + 1)
    tok, gau, acc, gacc, glow, res, in_sems, own_sems, gin_sems, gown_sems, out_sems, gout_sems = refs
    me, gauge_me = place[0], place[1]
    rows = arrays[0].shape[0]
    gauge_rows = gauges[0].shape[0]
    length = tok.shape[1]
    scaling = 1.0 / math.sqrt(HD)

    copies = []
    start = pl.multiple_of(me * columns + off, HD)
    for a in range(4):
        copies.append(
            pltpu.make_async_copy(
                arrays[a].at[:, pl.ds(start, width)],
                tok.at[a, pl.ds(pl.multiple_of(me * rows, rows), rows), :],
                own_sems.at[a],
            )
        )
    for at, k in enumerate(order):
        copies.append(
            pltpu.make_async_copy(
                recvs[at],
                tok.at[:, pl.ds(pl.multiple_of((me ^ k) * rows, rows), rows), :],
                in_sems.at[at],
            )
        )
    for a in range(2):
        copies.append(
            pltpu.make_async_copy(
                gauges[a].at[:, pl.ds(off, width)],
                gau.at[a, pl.ds(pl.multiple_of(gauge_me * gauge_rows, gauge_rows), gauge_rows), :],
                gown_sems.at[a],
            )
        )
    for at, k in enumerate(gauge_order):
        copies.append(
            pltpu.make_async_copy(
                gauge_recvs[at].at[:, :, pl.ds(off, width)],
                gau.at[
                    :, pl.ds(pl.multiple_of((gauge_me ^ k) * gauge_rows, gauge_rows), gauge_rows), :
                ],
                gin_sems.at[at],
            )
        )
    for copy in copies:
        copy.start()
    acc[...] = jnp.zeros_like(acc)
    gacc[...] = jnp.zeros_like(gacc)
    for copy in copies:
        copy.wait()

    def block(n, carry):
        here = pl.ds(pl.multiple_of(n * BLOCK, BLOCK), BLOCK)
        slots = [
            pl.ds(pl.multiple_of(lists[n, j] * BLOCK, BLOCK), BLOCK) for j in range(K_MAX)
        ]
        gslot = pl.ds(pl.multiple_of(chosen[n] * BLOCK, BLOCK), BLOCK)
        third = jnp.where(counts[n] == K_MAX, 0.0, -jnp.inf).astype(jnp.float32)
        base, listed = (K_MAX - 1) * BLOCK, K_MAX * BLOCK
        for h in range(width // HD):
            lanes = slice(h * HD, (h + 1) * HD)
            q = tok[0, here, lanes]
            g = tok[3, here, lanes]
            k = jnp.concatenate([tok[1, s, lanes] for s in slots] + [gau[0, gslot, lanes]], axis=0)
            v = jnp.concatenate([tok[2, s, lanes] for s in slots] + [gau[1, gslot, lanes]], axis=0)
            last = (((1,), (1,)), ((), ()))
            scores = lax.dot_general(k, q, last, preferred_element_type=jnp.float32)
            grad_probs = lax.dot_general(v, g, last, preferred_element_type=jnp.float32)
            scores = jnp.concatenate(
                [scores[:base], scores[base:listed] + third, scores[listed:]], axis=0
            )
            top = jnp.max(scores, axis=0, keepdims=True)
            weights = jnp.exp2((scores - top) * (scaling * math.log2(math.e)))
            inverse = 1.0 / jnp.sum(weights, axis=0, keepdims=True)
            delta = jnp.sum(weights * grad_probs, axis=0, keepdims=True) * inverse
            probs = weights * inverse
            grad_scores = (probs * ((grad_probs - delta) * scaling)).astype(jnp.bfloat16)
            probs_low = probs.astype(jnp.bfloat16)
            dk = jnp.dot(grad_scores, q, preferred_element_type=jnp.float32)
            dv = jnp.dot(probs_low, g, preferred_element_type=jnp.float32)
            res[0, here, lanes] = lax.dot_general(
                grad_scores, k, (((0,), (0,)), ((), ())), preferred_element_type=jnp.float32
            ).astype(jnp.bfloat16)
            for j in range(K_MAX):
                part = slice(j * BLOCK, (j + 1) * BLOCK)
                acc[0, slots[j], lanes] += dk[part]
                acc[1, slots[j], lanes] += dv[part]
            gacc[0, gslot, lanes] += dk[listed:]
            gacc[1, gslot, lanes] += dv[listed:]
        return carry

    lax.fori_loop(0, length // BLOCK, block, 0, unroll=4)

    glow[...] = gacc[...].astype(jnp.bfloat16)
    copies = []
    for at, k in enumerate((0,) + tuple(gauge_order)):
        part = pl.ds(pl.multiple_of((gauge_me ^ k) * gauge_rows, gauge_rows), gauge_rows)
        copies.append(
            pltpu.make_async_copy(
                (glow if k else gacc).at[:, part, :], gauge_outs[at], gout_sems.at[at]
            )
        )
    for copy in copies:
        copy.start()
    res[1] = acc[0].astype(jnp.bfloat16)
    res[2] = acc[1].astype(jnp.bfloat16)
    token_copies = []
    for at, (k, merged) in enumerate(targets):
        token_copies.append(
            pltpu.make_async_copy(
                res.at[:, pl.ds(pl.multiple_of((me ^ k) * rows, rows), rows), :],
                outs[at].at[:, :, pl.ds(off, width)] if merged else outs[at],
                out_sems.at[at],
            )
        )
    run_copies(token_copies)
    for copy in copies:
        copy.wait()


def unpack_kernel(columns, parts, place, *refs):
    outs, sems = refs[-4:-1], refs[-1]
    me = place[0]
    copies = []
    for at, (k, off, width) in enumerate(parts):
        start = pl.multiple_of((me ^ k) * columns + off, HD)
        for a in range(3):
            copies.append(
                pltpu.make_async_copy(
                    refs[at].at[a], outs[a].at[:, pl.ds(start, width)], sems.at[at, a]
                )
            )
    run_copies(copies)


def chunks_of(heads):
    if heads == 1:
        return [(0, HD)]
    half = heads // 2
    return [(0, half * HD), (half * HD, (heads - half) * HD)]


def local(
    sizes,
    queries,
    keys,
    values,
    grad_out,
    gauge_key,
    gauge_value,
    block_keys,
    block_count,
    gauge_block,
):
    total, head_total = sizes
    rows, model = queries.shape[1], queries.shape[2]
    gauge_rows = gauge_key.shape[0]
    length, gauge_total = rows * total, gauge_rows * head_total
    columns = model // total
    bf16, f32 = jnp.bfloat16, jnp.float32
    arrays = [x[0] for x in (queries, keys, values, grad_out)]
    arrays = [pltpu.with_memory_space_constraint(x, pltpu.HBM) for x in arrays]
    gauge_key, gauge_value = [
        pltpu.with_memory_space_constraint(x, pltpu.HBM) for x in (gauge_key, gauge_value)
    ]
    me = lax.axis_index(TOKENS).astype(jnp.int32)
    gauge_me = lax.axis_index("head").astype(jnp.int32)
    place = jnp.stack([me, gauge_me])
    half = total // 2
    order = tuple(k for i in range(half) for k in (total - 1 - i, half - 1 - i) if k)
    gauge_order = tuple(range(1, head_total))
    lists = (block_keys[0], block_count[0], gauge_block[0])
    params = pltpu.CompilerParams(vmem_limit_bytes=VMEM_LIMIT)

    def swap(x, axis, size, k):
        return lax.ppermute(x, axis, [(i, i ^ k) for i in range(size)])

    chunks = chunks_of(columns // HD)

    def pack(chunk, part, after, with_gauges):
        off, width = chunk
        shapes = [jax.ShapeDtypeStruct((4, rows, width), bf16)] * len(part)
        if with_gauges:
            shapes.append(jax.ShapeDtypeStruct((2, gauge_rows, columns), bf16))
        return pl.pallas_call(
            functools.partial(
                pack_kernel, off, width, columns, part, len(after), with_gauges
            ),
            out_shape=shapes,
            in_specs=[SMEM] + [ANY] * (6 + len(after)),
            out_specs=[ANY] * len(shapes),
            scratch_shapes=[
                pltpu.SemaphoreType.DMA((len(part), 4)),
                pltpu.SemaphoreType.DMA((2,)),
            ],
            compiler_params=params,
            name="pack",
        )(place, *arrays, gauge_key, gauge_value, *after)

    def grads(chunk, recvs, targets, held):
        off, width = chunk
        return pl.pallas_call(
            functools.partial(
                grads_kernel, off, width, columns, order, targets, gauge_order, 0, len(held)
            ),
            out_shape=[
                jax.ShapeDtypeStruct((3, rows, columns if merged else width), bf16)
                for _, merged in targets
            ]
            + [jax.ShapeDtypeStruct((2, gauge_rows, width), f32)]
            + [jax.ShapeDtypeStruct((2, gauge_rows, width), bf16)] * (head_total - 1),
            in_specs=[SMEM] * 4
            + [ANY] * (6 + len(order) + len(gauge_order) + len(held)),
            out_specs=[ANY] * (total + head_total),
            scratch_shapes=[
                pltpu.VMEM((4, length, width), bf16),
                pltpu.VMEM((2, gauge_total, width), bf16),
                pltpu.VMEM((2, length, width), f32),
                pltpu.VMEM((2, gauge_total, width), f32),
                pltpu.VMEM((2, gauge_total, width), bf16),
                pltpu.VMEM((3, length, width), bf16),
                pltpu.SemaphoreType.DMA((max(len(order), 1),)),
                pltpu.SemaphoreType.DMA((4,)),
                pltpu.SemaphoreType.DMA((max(len(gauge_order), 1),)),
                pltpu.SemaphoreType.DMA((2,)),
                pltpu.SemaphoreType.DMA((total,)),
                pltpu.SemaphoreType.DMA((head_total,)),
            ],
            compiler_params=params,
            cost_estimate=pl.CostEstimate(
                flops=10 * (K_MAX + 1) * BLOCK * length * width * 16,
                bytes_accessed=14 * length * width,
                transcendentals=0,
            ),
            input_output_aliases={
                10 + len(order) + len(gauge_order) + i: i for i in range(len(held))
            },
            name="grads",
        )(place, *lists, *arrays, gauge_key, gauge_value, *recvs, *gauge_recvs, *held)

    def hold(buffers, after):
        return pl.pallas_call(
            lambda *refs: None,
            out_shape=[jax.ShapeDtypeStruct(x.shape, x.dtype) for x in buffers],
            in_specs=[ANY] * (len(buffers) + len(after)),
            out_specs=[ANY] * len(buffers),
            input_output_aliases={i: i for i in range(len(buffers))},
            compiler_params=params,
            name="hold",
        )(*buffers, *after)

    def unpack(parts, outs, after):
        held = len(outs)
        return pl.pallas_call(
            functools.partial(unpack_kernel, columns, [part[1:] for part in parts]),
            out_shape=[jax.ShapeDtypeStruct((rows, model), bf16)] * 3,
            in_specs=[SMEM] + [ANY] * (len(parts) + held + len(after)),
            out_specs=[ANY] * 3,
            scratch_shapes=[pltpu.SemaphoreType.DMA((len(parts), 3))],
            input_output_aliases={1 + len(parts) + i: i for i in range(held)},
            compiler_params=params,
            name="unpack",
        )(place, *[part[0] for part in parts], *outs, *after)

    def send(packed, part):
        return [swap(s, TOKENS, total, k) for s, k in zip(packed, part)]

    single = len(chunks) == 1
    *packed, gauge_send = pack(chunks[0], order, [], True)
    gauge_recvs = [swap(gauge_send, "head", head_total, k) for k in gauge_order]
    recvs = send(packed, order)
    early = () if single else order[0 : 2 * EARLY : 2]
    far, near = order[0::2], order[1::2]
    whole = (*far[2:3], *near[:2], *far[3:], *near[2:]) if early else order
    targets = tuple((k, True) for k in (0, *whole)) + tuple((k, False) for k in early)
    merged, parts, gauge_sums, back_early = [], [], [], []
    for at, chunk in enumerate(chunks):
        ahead = []
        if at + 1 < len(chunks):
            ahead = send(pack(chunks[at + 1], order, recvs[:1], False), order)
        out = grads(chunk, recvs, targets, merged)
        if gauge_sums:
            out = hold(out, back_early[:1] + gauge_back)
        merged, cut = list(out[: 1 + len(whole)]), out[1 + len(whole) : total]
        if at + 1 < len(chunks):
            cut = hold(cut, ahead[:EHOLD])
            back_early = send(cut, early)
            parts += [(x, k, *chunk) for x, k in zip(back_early, early)]
        gauge_back = [
            swap(x, "head", head_total, k) for x, k in zip(out[total + 1 :], gauge_order)
        ]
        gauge_sums.append(sum((x.astype(f32) for x in gauge_back), out[total]))
        recvs = ahead
    pieces = dict(zip(whole, merged[1:]))
    late = [(swap(pieces[k], TOKENS, total, k), k, 0, columns) for k in whole]
    if early:
        late = [(x, k, *chunks[-1]) for x, k in zip(send(cut, early), early)] + late
    gauge_sum = jnp.concatenate(gauge_sums, axis=2)
    gauge_grads = [gauge_sum[0], gauge_sum[1]]
    parts = parts + [(merged[0], 0, 0, columns)] + late
    outs = unpack(parts[:-TAIL], [], [])
    outs = unpack(parts[-TAIL:], outs, gauge_grads)
    return (outs[0][None], outs[1][None], outs[2][None], *gauge_grads)


def solution(mesh):
    tokens = P(("groups", "head"), TOKENS, None)
    gauges = P(("groups", "head"), TOKENS)
    lists = P(("groups", "head"), None, None)
    counts = P(("groups", "head"), None)
    sizes = (mesh.shape["seq"] * mesh.shape["rep"], mesh.shape["head"])
    return jax.shard_map(
        functools.partial(local, sizes),
        mesh=mesh,
        in_specs=(tokens,) * 4 + (gauges,) * 2 + (lists, counts, counts),
        out_specs=(tokens,) * 3 + (gauges,) * 2,
        check_vma=False,
    )
```

```python
import functools
import math

import jax
import jax.numpy as jnp
from jax import lax
from jax.experimental import pallas as pl
from jax.experimental.pallas import tpu as pltpu
from jax.sharding import PartitionSpec as P

HD = 128
BLOCK = 128
K_MAX = 3
EARLY = 2
EHOLD = 5
TAIL = 3
FIRST = 1
TOKENS = ("seq", "rep")
ANY = pl.BlockSpec(memory_space=pl.ANY)
SMEM = pl.BlockSpec(memory_space=pltpu.SMEM)
VMEM_LIMIT = 16 * 1024 * 1024


def run_copies(copies):
    for copy in copies:
        copy.start()
    for copy in copies:
        copy.wait()


def pack_kernel(off, width, columns, order, waits, with_gauges, place, *refs):
    arrays, gauges = refs[0:4], refs[4:6]
    sends = refs[6 + waits : 6 + waits + len(order)]
    sems, gauge_sems = refs[-2:]
    me = place[0]
    copies = []
    for at, k in enumerate(order):
        start = pl.multiple_of((me ^ k) * columns + off, HD)
        for a in range(4):
            copies.append(
                pltpu.make_async_copy(
                    arrays[a].at[:, pl.ds(start, width)], sends[at].at[a], sems.at[at, a]
                )
            )
    if with_gauges:
        for a in range(2):
            copies.append(
                pltpu.make_async_copy(
                    gauges[a].at[:, pl.ds(off, width)], refs[-3].at[a], gauge_sems.at[a]
                )
            )
    run_copies(copies)


def grads_kernel(
    off, width, columns, order, targets, gauge_order, waits, held, place, lists, counts, chosen, *refs
):
    n_tok, n_gauge = len(order), len(gauge_order)
    refs = list(refs)

    def take(count):
        out = refs[:count]
        del refs[:count]
        return out

    arrays, gauges = take(4), take(2)
    recvs, gauge_recvs = take(n_tok), take(n_gauge)
    take(waits + held)
    outs, gauge_outs = take(n_tok + 1), take(n_gauge + 1)
    tok, gau, acc, gacc, glow, res, in_sems, own_sems, gin_sems, gown_sems, out_sems, gout_sems = refs
    me, gauge_me = place[0], place[1]
    rows = arrays[0].shape[0]
    gauge_rows = gauges[0].shape[0]
    length = tok.shape[1]
    scaling = 1.0 / math.sqrt(HD)

    copies = []
    start = pl.multiple_of(me * columns + off, HD)
    for a in range(4):
        copies.append(
            pltpu.make_async_copy(
                arrays[a].at[:, pl.ds(start, width)],
                tok.at[a, pl.ds(pl.multiple_of(me * rows, rows), rows), :],
                own_sems.at[a],
            )
        )
    for at, k in enumerate(order):
        copies.append(
            pltpu.make_async_copy(
                recvs[at],
                tok.at[:, pl.ds(pl.multiple_of((me ^ k) * rows, rows), rows), :],
                in_sems.at[at],
            )
        )
    for a in range(2):
        copies.append(
            pltpu.make_async_copy(
                gauges[a].at[:, pl.ds(off, width)],
                gau.at[a, pl.ds(pl.multiple_of(gauge_me * gauge_rows, gauge_rows), gauge_rows), :],
                gown_sems.at[a],
            )
        )
    for at, k in enumerate(gauge_order):
        copies.append(
            pltpu.make_async_copy(
                gauge_recvs[at],
                gau.at[
                    :, pl.ds(pl.multiple_of((gauge_me ^ k) * gauge_rows, gauge_rows), gauge_rows), :
                ],
                gin_sems.at[at],
            )
        )
    for copy in copies:
        copy.start()
    acc[...] = jnp.zeros_like(acc)
    gacc[...] = jnp.zeros_like(gacc)
    for copy in copies:
        copy.wait()

    def block(n, carry):
        here = pl.ds(pl.multiple_of(n * BLOCK, BLOCK), BLOCK)
        slots = [
            pl.ds(pl.multiple_of(lists[n, j] * BLOCK, BLOCK), BLOCK) for j in range(K_MAX)
        ]
        gslot = pl.ds(pl.multiple_of(chosen[n] * BLOCK, BLOCK), BLOCK)
        third = jnp.where(counts[n] == K_MAX, 0.0, -jnp.inf).astype(jnp.float32)
        base, listed = (K_MAX - 1) * BLOCK, K_MAX * BLOCK
        for h in range(width // HD):
            lanes = slice(h * HD, (h + 1) * HD)
            q = tok[0, here, lanes]
            g = tok[3, here, lanes]
            k = jnp.concatenate([tok[1, s, lanes] for s in slots] + [gau[0, gslot, lanes]], axis=0)
            v = jnp.concatenate([tok[2, s, lanes] for s in slots] + [gau[1, gslot, lanes]], axis=0)
            last = (((1,), (1,)), ((), ()))
            scores = lax.dot_general(k, q, last, preferred_element_type=jnp.float32)
            grad_probs = lax.dot_general(v, g, last, preferred_element_type=jnp.float32)
            scores = jnp.concatenate(
                [scores[:base], scores[base:listed] + third, scores[listed:]], axis=0
            )
            top = jnp.max(scores, axis=0, keepdims=True)
            weights = jnp.exp2((scores - top) * (scaling * math.log2(math.e)))
            inverse = 1.0 / jnp.sum(weights, axis=0, keepdims=True)
            delta = jnp.sum(weights * grad_probs, axis=0, keepdims=True) * inverse
            probs = weights * inverse
            grad_scores = (probs * ((grad_probs - delta) * scaling)).astype(jnp.bfloat16)
            probs_low = probs.astype(jnp.bfloat16)
            dk = jnp.dot(grad_scores, q, preferred_element_type=jnp.float32)
            dv = jnp.dot(probs_low, g, preferred_element_type=jnp.float32)
            res[0, here, lanes] = lax.dot_general(
                grad_scores, k, (((0,), (0,)), ((), ())), preferred_element_type=jnp.float32
            ).astype(jnp.bfloat16)
            for j in range(K_MAX):
                part = slice(j * BLOCK, (j + 1) * BLOCK)
                acc[0, slots[j], lanes] += dk[part]
                acc[1, slots[j], lanes] += dv[part]
            gacc[0, gslot, lanes] += dk[listed:]
            gacc[1, gslot, lanes] += dv[listed:]
        return carry

    lax.fori_loop(0, length // BLOCK, block, 0, unroll=4)

    glow[...] = gacc[...].astype(jnp.bfloat16)
    copies = []
    for at, k in enumerate((0,) + tuple(gauge_order)):
        part = pl.ds(pl.multiple_of((gauge_me ^ k) * gauge_rows, gauge_rows), gauge_rows)
        copies.append(
            pltpu.make_async_copy(
                (glow if k else gacc).at[:, part, :], gauge_outs[at], gout_sems.at[at]
            )
        )
    for copy in copies:
        copy.start()
    res[1] = acc[0].astype(jnp.bfloat16)
    res[2] = acc[1].astype(jnp.bfloat16)
    token_copies = []
    for at, (k, merged) in enumerate(targets):
        token_copies.append(
            pltpu.make_async_copy(
                res.at[:, pl.ds(pl.multiple_of((me ^ k) * rows, rows), rows), :],
                outs[at].at[:, :, pl.ds(off, width)] if merged else outs[at],
                out_sems.at[at],
            )
        )
    run_copies(token_copies)
    for copy in copies:
        copy.wait()


def unpack_kernel(columns, parts, place, *refs):
    outs, sems = refs[-4:-1], refs[-1]
    me = place[0]
    copies = []
    for at, (k, off, width) in enumerate(parts):
        start = pl.multiple_of((me ^ k) * columns + off, HD)
        for a in range(3):
            copies.append(
                pltpu.make_async_copy(
                    refs[at].at[a], outs[a].at[:, pl.ds(start, width)], sems.at[at, a]
                )
            )
    run_copies(copies)


def chunks_of(heads):
    if heads == 1:
        return [(0, HD)]
    half = heads // 2
    return [(0, half * HD), (half * HD, (heads - half) * HD)]


def local(
    sizes,
    queries,
    keys,
    values,
    grad_out,
    gauge_key,
    gauge_value,
    block_keys,
    block_count,
    gauge_block,
):
    total, head_total = sizes
    rows, model = queries.shape[1], queries.shape[2]
    gauge_rows = gauge_key.shape[0]
    length, gauge_total = rows * total, gauge_rows * head_total
    columns = model // total
    bf16, f32 = jnp.bfloat16, jnp.float32
    arrays = [x[0] for x in (queries, keys, values, grad_out)]
    arrays = [pltpu.with_memory_space_constraint(x, pltpu.HBM) for x in arrays]
    gauge_key, gauge_value = [
        pltpu.with_memory_space_constraint(x, pltpu.HBM) for x in (gauge_key, gauge_value)
    ]
    me = lax.axis_index(TOKENS).astype(jnp.int32)
    gauge_me = lax.axis_index("head").astype(jnp.int32)
    place = jnp.stack([me, gauge_me])
    half = total // 2
    far, near = list(range(total - 1, half - 1, -1)), list(range(half - 1, -1, -1))
    far[:2] = far[1::-1]
    order = tuple(k for pair in zip(far, near) for k in pair if k)
    gauge_order = tuple(range(1, head_total))
    lists = (block_keys[0], block_count[0], gauge_block[0])
    params = pltpu.CompilerParams(vmem_limit_bytes=VMEM_LIMIT)

    def swap(x, axis, size, k):
        return lax.ppermute(x, axis, [(i, i ^ k) for i in range(size)])

    chunks = chunks_of(columns // HD)

    def pack(chunk, part, after, with_gauges):
        off, width = chunk
        shapes = [jax.ShapeDtypeStruct((4, rows, width), bf16)] * len(part)
        if with_gauges:
            shapes.append(jax.ShapeDtypeStruct((2, gauge_rows, width), bf16))
        return pl.pallas_call(
            functools.partial(
                pack_kernel, off, width, columns, part, len(after), with_gauges
            ),
            out_shape=shapes,
            in_specs=[SMEM] + [ANY] * (6 + len(after)),
            out_specs=[ANY] * len(shapes),
            scratch_shapes=[
                pltpu.SemaphoreType.DMA((max(len(part), 1), 4)),
                pltpu.SemaphoreType.DMA((2,)),
            ],
            compiler_params=params,
            name="pack",
        )(place, *arrays, gauge_key, gauge_value, *after)

    def grads(chunk, recvs, gauge_recvs, targets, held):
        off, width = chunk
        return pl.pallas_call(
            functools.partial(
                grads_kernel, off, width, columns, order, targets, gauge_order, 0, len(held)
            ),
            out_shape=[
                jax.ShapeDtypeStruct((3, rows, columns if merged else width), bf16)
                for _, merged in targets
            ]
            + [jax.ShapeDtypeStruct((2, gauge_rows, width), f32)]
            + [jax.ShapeDtypeStruct((2, gauge_rows, width), bf16)] * (head_total - 1),
            in_specs=[SMEM] * 4
            + [ANY] * (6 + len(order) + len(gauge_order) + len(held)),
            out_specs=[ANY] * (total + head_total),
            scratch_shapes=[
                pltpu.VMEM((4, length, width), bf16),
                pltpu.VMEM((2, gauge_total, width), bf16),
                pltpu.VMEM((2, length, width), f32),
                pltpu.VMEM((2, gauge_total, width), f32),
                pltpu.VMEM((2, gauge_total, width), bf16),
                pltpu.VMEM((3, length, width), bf16),
                pltpu.SemaphoreType.DMA((max(len(order), 1),)),
                pltpu.SemaphoreType.DMA((4,)),
                pltpu.SemaphoreType.DMA((max(len(gauge_order), 1),)),
                pltpu.SemaphoreType.DMA((2,)),
                pltpu.SemaphoreType.DMA((total,)),
                pltpu.SemaphoreType.DMA((head_total,)),
            ],
            compiler_params=params,
            cost_estimate=pl.CostEstimate(
                flops=10 * (K_MAX + 1) * BLOCK * length * width * 16,
                bytes_accessed=14 * length * width,
                transcendentals=0,
            ),
            input_output_aliases={
                10 + len(order) + len(gauge_order) + i: i for i in range(len(held))
            },
            name="grads",
        )(place, *lists, *arrays, gauge_key, gauge_value, *recvs, *gauge_recvs, *held)

    def hold(buffers, after):
        return pl.pallas_call(
            lambda *refs: None,
            out_shape=[jax.ShapeDtypeStruct(x.shape, x.dtype) for x in buffers],
            in_specs=[ANY] * (len(buffers) + len(after)),
            out_specs=[ANY] * len(buffers),
            input_output_aliases={i: i for i in range(len(buffers))},
            compiler_params=params,
            name="hold",
        )(*buffers, *after)

    def unpack(parts, outs, after):
        held = len(outs)
        return pl.pallas_call(
            functools.partial(unpack_kernel, columns, [part[1:] for part in parts]),
            out_shape=[jax.ShapeDtypeStruct((rows, model), bf16)] * 3,
            in_specs=[SMEM] + [ANY] * (len(parts) + held + len(after)),
            out_specs=[ANY] * 3,
            scratch_shapes=[pltpu.SemaphoreType.DMA((len(parts), 3))],
            input_output_aliases={1 + len(parts) + i: i for i in range(held)},
            compiler_params=params,
            name="unpack",
        )(place, *[part[0] for part in parts], *outs, *after)

    def send(packed, part):
        return [swap(s, TOKENS, total, k) for s, k in zip(packed, part)]

    single = len(chunks) == 1
    packed = list(pack(chunks[0], order[:FIRST], [], False))
    packed += pack(chunks[0], order[FIRST:], packed[:1], False)
    recvs = send(packed, order)
    early = () if single else tuple(far[:EARLY])
    rest = [k for k in near if k]
    whole = (*far[2:3], *rest[:2], *far[3:], *rest[2:]) if early else order
    targets = tuple((k, True) for k in (0, *whole)) + tuple((k, False) for k in early)
    merged, parts, gauge_sums, back_early = [], [], [], []
    for at, chunk in enumerate(chunks):
        ahead = []
        if at + 1 < len(chunks):
            ahead = send(pack(chunks[at + 1], order, recvs[:1], False), order)
        (gauge_send,) = pack(chunk, (), [], True)
        gauge_recvs = [swap(gauge_send, "head", head_total, k) for k in gauge_order]
        out = grads(chunk, recvs, gauge_recvs, targets, merged)
        if gauge_sums:
            out = hold(out, back_early[:1] + gauge_back)
        merged, cut = list(out[: 1 + len(whole)]), out[1 + len(whole) : total]
        if at + 1 < len(chunks):
            cut = hold(cut, ahead[:EHOLD])
            back_early = send(cut, early)
            parts += [(x, k, *chunk) for x, k in zip(back_early, early)]
        gauge_back = [
            swap(x, "head", head_total, k) for x, k in zip(out[total + 1 :], gauge_order)
        ]
        gauge_sums.append(sum((x.astype(f32) for x in gauge_back), out[total]))
        recvs = ahead
    pieces = dict(zip(whole, merged[1:]))
    late = [(swap(pieces[k], TOKENS, total, k), k, 0, columns) for k in whole]
    if early:
        late = [(x, k, *chunks[-1]) for x, k in zip(send(cut, early), early)] + late
    gauge_sum = jnp.concatenate(gauge_sums, axis=2)
    gauge_grads = [gauge_sum[0], gauge_sum[1]]
    parts = parts + [(merged[0], 0, 0, columns)] + late
    outs = unpack(parts[:-TAIL], [], [])
    outs = unpack(parts[-TAIL:], outs, gauge_grads)
    return (outs[0][None], outs[1][None], outs[2][None], *gauge_grads)


def solution(mesh):
    tokens = P(("groups", "head"), TOKENS, None)
    gauges = P(("groups", "head"), TOKENS)
    lists = P(("groups", "head"), None, None)
    counts = P(("groups", "head"), None)
    sizes = (mesh.shape["seq"] * mesh.shape["rep"], mesh.shape["head"])
    return jax.shard_map(
        functools.partial(local, sizes),
        mesh=mesh,
        in_specs=(tokens,) * 4 + (gauges,) * 2 + (lists, counts, counts),
        out_specs=(tokens,) * 3 + (gauges,) * 2,
        check_vma=False,
    )
```

```python
import functools
import math

import jax
import jax.numpy as jnp
from jax import lax
from jax.experimental import pallas as pl
from jax.experimental.pallas import tpu as pltpu
from jax.sharding import PartitionSpec as P

HD = 128
BLOCK = 128
K_MAX = 3
EARLY = 3
EHOLD = 5
TAIL = 3
FIRST = 1
TOKENS = ("seq", "rep")
ANY = pl.BlockSpec(memory_space=pl.ANY)
SMEM = pl.BlockSpec(memory_space=pltpu.SMEM)
VMEM_LIMIT = 16 * 1024 * 1024


def run_copies(copies):
    for copy in copies:
        copy.start()
    for copy in copies:
        copy.wait()


def pack_kernel(off, width, columns, order, waits, with_gauges, place, *refs):
    arrays, gauges = refs[0:4], refs[4:6]
    sends = refs[6 + waits : 6 + waits + len(order)]
    sems, gauge_sems = refs[-2:]
    me = place[0]
    copies = []
    for at, k in enumerate(order):
        start = pl.multiple_of((me ^ k) * columns + off, HD)
        for a in range(4):
            copies.append(
                pltpu.make_async_copy(
                    arrays[a].at[:, pl.ds(start, width)], sends[at].at[a], sems.at[at, a]
                )
            )
    if with_gauges:
        for a in range(2):
            copies.append(
                pltpu.make_async_copy(
                    gauges[a].at[:, pl.ds(off, width)], refs[-3].at[a], gauge_sems.at[a]
                )
            )
    run_copies(copies)


def grads_kernel(
    off, width, columns, order, targets, gauge_order, waits, held, place, lists, counts, chosen, *refs
):
    n_tok, n_gauge = len(order), len(gauge_order)
    refs = list(refs)

    def take(count):
        out = refs[:count]
        del refs[:count]
        return out

    arrays, gauges = take(4), take(2)
    recvs, gauge_recvs = take(n_tok), take(n_gauge)
    take(waits + held)
    outs, gauge_outs = take(n_tok + 1), take(n_gauge + 1)
    tok, gau, acc, gacc, glow, res, in_sems, own_sems, gin_sems, gown_sems, out_sems, gout_sems = refs
    me, gauge_me = place[0], place[1]
    rows = arrays[0].shape[0]
    gauge_rows = gauges[0].shape[0]
    length = tok.shape[1]
    scaling = 1.0 / math.sqrt(HD)

    copies = []
    start = pl.multiple_of(me * columns + off, HD)
    for a in range(4):
        copies.append(
            pltpu.make_async_copy(
                arrays[a].at[:, pl.ds(start, width)],
                tok.at[a, pl.ds(pl.multiple_of(me * rows, rows), rows), :],
                own_sems.at[a],
            )
        )
    for at, k in enumerate(order):
        copies.append(
            pltpu.make_async_copy(
                recvs[at],
                tok.at[:, pl.ds(pl.multiple_of((me ^ k) * rows, rows), rows), :],
                in_sems.at[at],
            )
        )
    for a in range(2):
        copies.append(
            pltpu.make_async_copy(
                gauges[a].at[:, pl.ds(off, width)],
                gau.at[a, pl.ds(pl.multiple_of(gauge_me * gauge_rows, gauge_rows), gauge_rows), :],
                gown_sems.at[a],
            )
        )
    for at, k in enumerate(gauge_order):
        copies.append(
            pltpu.make_async_copy(
                gauge_recvs[at],
                gau.at[
                    :, pl.ds(pl.multiple_of((gauge_me ^ k) * gauge_rows, gauge_rows), gauge_rows), :
                ],
                gin_sems.at[at],
            )
        )
    for copy in copies:
        copy.start()
    acc[...] = jnp.zeros_like(acc)
    gacc[...] = jnp.zeros_like(gacc)
    for copy in copies:
        copy.wait()

    def block(n, carry):
        here = pl.ds(pl.multiple_of(n * BLOCK, BLOCK), BLOCK)
        slots = [
            pl.ds(pl.multiple_of(lists[n, j] * BLOCK, BLOCK), BLOCK) for j in range(K_MAX)
        ]
        gslot = pl.ds(pl.multiple_of(chosen[n] * BLOCK, BLOCK), BLOCK)
        third = jnp.where(counts[n] == K_MAX, 0.0, -jnp.inf).astype(jnp.float32)
        base, listed = (K_MAX - 1) * BLOCK, K_MAX * BLOCK
        for h in range(width // HD):
            lanes = slice(h * HD, (h + 1) * HD)
            q = tok[0, here, lanes]
            g = tok[3, here, lanes]
            k = jnp.concatenate([tok[1, s, lanes] for s in slots] + [gau[0, gslot, lanes]], axis=0)
            v = jnp.concatenate([tok[2, s, lanes] for s in slots] + [gau[1, gslot, lanes]], axis=0)
            last = (((1,), (1,)), ((), ()))
            scores = lax.dot_general(k, q, last, preferred_element_type=jnp.float32)
            grad_probs = lax.dot_general(v, g, last, preferred_element_type=jnp.float32)
            scores = jnp.concatenate(
                [scores[:base], scores[base:listed] + third, scores[listed:]], axis=0
            )
            top = jnp.max(scores, axis=0, keepdims=True)
            weights = jnp.exp2((scores - top) * (scaling * math.log2(math.e)))
            inverse = 1.0 / jnp.sum(weights, axis=0, keepdims=True)
            delta = jnp.sum(weights * grad_probs, axis=0, keepdims=True) * inverse
            probs = weights * inverse
            grad_scores = (probs * ((grad_probs - delta) * scaling)).astype(jnp.bfloat16)
            probs_low = probs.astype(jnp.bfloat16)
            dk = jnp.dot(grad_scores, q, preferred_element_type=jnp.float32)
            dv = jnp.dot(probs_low, g, preferred_element_type=jnp.float32)
            res[0, here, lanes] = lax.dot_general(
                grad_scores, k, (((0,), (0,)), ((), ())), preferred_element_type=jnp.float32
            ).astype(jnp.bfloat16)
            for j in range(K_MAX):
                part = slice(j * BLOCK, (j + 1) * BLOCK)
                acc[0, slots[j], lanes] += dk[part]
                acc[1, slots[j], lanes] += dv[part]
            gacc[0, gslot, lanes] += dk[listed:]
            gacc[1, gslot, lanes] += dv[listed:]
        return carry

    lax.fori_loop(0, length // BLOCK, block, 0, unroll=4)

    glow[...] = gacc[...].astype(jnp.bfloat16)
    copies = []
    for at, k in enumerate((0,) + tuple(gauge_order)):
        part = pl.ds(pl.multiple_of((gauge_me ^ k) * gauge_rows, gauge_rows), gauge_rows)
        copies.append(
            pltpu.make_async_copy(
                (glow if k else gacc).at[:, part, :], gauge_outs[at], gout_sems.at[at]
            )
        )
    for copy in copies:
        copy.start()
    res[1] = acc[0].astype(jnp.bfloat16)
    res[2] = acc[1].astype(jnp.bfloat16)
    token_copies = []
    for at, (k, merged) in enumerate(targets):
        token_copies.append(
            pltpu.make_async_copy(
                res.at[:, pl.ds(pl.multiple_of((me ^ k) * rows, rows), rows), :],
                outs[at].at[:, :, pl.ds(off, width)] if merged else outs[at],
                out_sems.at[at],
            )
        )
    run_copies(token_copies)
    for copy in copies:
        copy.wait()


def unpack_kernel(columns, parts, place, *refs):
    outs, sems = refs[-4:-1], refs[-1]
    me = place[0]
    copies = []
    for at, (k, off, width) in enumerate(parts):
        start = pl.multiple_of((me ^ k) * columns + off, HD)
        for a in range(3):
            copies.append(
                pltpu.make_async_copy(
                    refs[at].at[a], outs[a].at[:, pl.ds(start, width)], sems.at[at, a]
                )
            )
    run_copies(copies)


def chunks_of(heads):
    if heads == 1:
        return [(0, HD)]
    half = heads // 2
    return [(0, half * HD), (half * HD, (heads - half) * HD)]


def local(
    sizes,
    queries,
    keys,
    values,
    grad_out,
    gauge_key,
    gauge_value,
    block_keys,
    block_count,
    gauge_block,
):
    total, head_total = sizes
    rows, model = queries.shape[1], queries.shape[2]
    gauge_rows = gauge_key.shape[0]
    length, gauge_total = rows * total, gauge_rows * head_total
    columns = model // total
    bf16, f32 = jnp.bfloat16, jnp.float32
    arrays = [x[0] for x in (queries, keys, values, grad_out)]
    arrays = [pltpu.with_memory_space_constraint(x, pltpu.HBM) for x in arrays]
    gauge_key, gauge_value = [
        pltpu.with_memory_space_constraint(x, pltpu.HBM) for x in (gauge_key, gauge_value)
    ]
    me = lax.axis_index(TOKENS).astype(jnp.int32)
    gauge_me = lax.axis_index("head").astype(jnp.int32)
    place = jnp.stack([me, gauge_me])
    half = total // 2
    far, near = list(range(total - 1, half - 1, -1)), list(range(half - 1, -1, -1))
    far[:2] = far[1::-1]
    order = tuple(k for pair in zip(far, near) for k in pair if k)
    gauge_order = tuple(range(1, head_total))
    lists = (block_keys[0], block_count[0], gauge_block[0])
    params = pltpu.CompilerParams(vmem_limit_bytes=VMEM_LIMIT)

    def swap(x, axis, size, k):
        return lax.ppermute(x, axis, [(i, i ^ k) for i in range(size)])

    chunks = chunks_of(columns // HD)

    def pack(chunk, part, after, with_gauges):
        off, width = chunk
        shapes = [jax.ShapeDtypeStruct((4, rows, width), bf16)] * len(part)
        if with_gauges:
            shapes.append(jax.ShapeDtypeStruct((2, gauge_rows, width), bf16))
        return pl.pallas_call(
            functools.partial(
                pack_kernel, off, width, columns, part, len(after), with_gauges
            ),
            out_shape=shapes,
            in_specs=[SMEM] + [ANY] * (6 + len(after)),
            out_specs=[ANY] * len(shapes),
            scratch_shapes=[
                pltpu.SemaphoreType.DMA((max(len(part), 1), 4)),
                pltpu.SemaphoreType.DMA((2,)),
            ],
            compiler_params=params,
            name="pack",
        )(place, *arrays, gauge_key, gauge_value, *after)

    def grads(chunk, recvs, gauge_recvs, targets, held):
        off, width = chunk
        return pl.pallas_call(
            functools.partial(
                grads_kernel, off, width, columns, order, targets, gauge_order, 0, len(held)
            ),
            out_shape=[
                jax.ShapeDtypeStruct((3, rows, columns if merged else width), bf16)
                for _, merged in targets
            ]
            + [jax.ShapeDtypeStruct((2, gauge_rows, width), f32)]
            + [jax.ShapeDtypeStruct((2, gauge_rows, width), bf16)] * (head_total - 1),
            in_specs=[SMEM] * 4
            + [ANY] * (6 + len(order) + len(gauge_order) + len(held)),
            out_specs=[ANY] * (total + head_total),
            scratch_shapes=[
                pltpu.VMEM((4, length, width), bf16),
                pltpu.VMEM((2, gauge_total, width), bf16),
                pltpu.VMEM((2, length, width), f32),
                pltpu.VMEM((2, gauge_total, width), f32),
                pltpu.VMEM((2, gauge_total, width), bf16),
                pltpu.VMEM((3, length, width), bf16),
                pltpu.SemaphoreType.DMA((max(len(order), 1),)),
                pltpu.SemaphoreType.DMA((4,)),
                pltpu.SemaphoreType.DMA((max(len(gauge_order), 1),)),
                pltpu.SemaphoreType.DMA((2,)),
                pltpu.SemaphoreType.DMA((total,)),
                pltpu.SemaphoreType.DMA((head_total,)),
            ],
            compiler_params=params,
            cost_estimate=pl.CostEstimate(
                flops=10 * (K_MAX + 1) * BLOCK * length * width * 16,
                bytes_accessed=14 * length * width,
                transcendentals=0,
            ),
            input_output_aliases={
                10 + len(order) + len(gauge_order) + i: i for i in range(len(held))
            },
            name="grads",
        )(place, *lists, *arrays, gauge_key, gauge_value, *recvs, *gauge_recvs, *held)

    def hold(buffers, after):
        return pl.pallas_call(
            lambda *refs: None,
            out_shape=[jax.ShapeDtypeStruct(x.shape, x.dtype) for x in buffers],
            in_specs=[ANY] * (len(buffers) + len(after)),
            out_specs=[ANY] * len(buffers),
            input_output_aliases={i: i for i in range(len(buffers))},
            compiler_params=params,
            name="hold",
        )(*buffers, *after)

    def unpack(parts, outs, after):
        held = len(outs)
        return pl.pallas_call(
            functools.partial(unpack_kernel, columns, [part[1:] for part in parts]),
            out_shape=[jax.ShapeDtypeStruct((rows, model), bf16)] * 3,
            in_specs=[SMEM] + [ANY] * (len(parts) + held + len(after)),
            out_specs=[ANY] * 3,
            scratch_shapes=[pltpu.SemaphoreType.DMA((len(parts), 3))],
            input_output_aliases={1 + len(parts) + i: i for i in range(held)},
            compiler_params=params,
            name="unpack",
        )(place, *[part[0] for part in parts], *outs, *after)

    def send(packed, part):
        return [swap(s, TOKENS, total, k) for s, k in zip(packed, part)]

    single = len(chunks) == 1
    packed = list(pack(chunks[0], order[:FIRST], [], False))
    packed += pack(chunks[0], order[FIRST:], packed[:1], False)
    recvs = send(packed, order)
    early = () if single else tuple(far[:EARLY])
    rest = [k for k in near if k]
    whole = (*far[EARLY:], *rest) if early else order
    targets = tuple((k, True) for k in (0, *whole)) + tuple((k, False) for k in early)
    merged, parts, gauge_sums, back_early = [], [], [], []
    for at, chunk in enumerate(chunks):
        ahead = []
        if at + 1 < len(chunks):
            ahead = send(pack(chunks[at + 1], order, recvs[:1], False), order)
        (gauge_send,) = pack(chunk, (), [], True)
        gauge_recvs = [swap(gauge_send, "head", head_total, k) for k in gauge_order]
        out = grads(chunk, recvs, gauge_recvs, targets, merged)
        if gauge_sums:
            out = hold(out, back_early[:1] + gauge_back)
        merged, cut = list(out[: 1 + len(whole)]), out[1 + len(whole) : total]
        if at + 1 < len(chunks):
            cut = hold(cut, ahead[:EHOLD])
            back_early = send(cut, early)
            parts += [(x, k, *chunk) for x, k in zip(back_early, early)]
        gauge_back = [
            swap(x, "head", head_total, k) for x, k in zip(out[total + 1 :], gauge_order)
        ]
        gauge_sums.append(sum((x.astype(f32) for x in gauge_back), out[total]))
        recvs = ahead
    pieces = dict(zip(whole, merged[1:]))
    late = [(swap(pieces[k], TOKENS, total, k), k, 0, columns) for k in whole]
    if early:
        cuts = [(x, k, *chunks[-1]) for x, k in zip(send(cut, early), early)]
        late = [cuts[0], late[1], cuts[1], late[0], late[2], cuts[2], *late[3:]]
    gauge_sum = jnp.concatenate(gauge_sums, axis=2)
    gauge_grads = [gauge_sum[0], gauge_sum[1]]
    parts = parts + [(merged[0], 0, 0, columns)] + late
    outs = unpack(parts[:-TAIL], [], [])
    outs = unpack(parts[-TAIL:], outs, gauge_grads)
    return (outs[0][None], outs[1][None], outs[2][None], *gauge_grads)


def solution(mesh):
    tokens = P(("groups", "head"), TOKENS, None)
    gauges = P(("groups", "head"), TOKENS)
    lists = P(("groups", "head"), None, None)
    counts = P(("groups", "head"), None)
    sizes = (mesh.shape["seq"] * mesh.shape["rep"], mesh.shape["head"])
    return jax.shard_map(
        functools.partial(local, sizes),
        mesh=mesh,
        in_specs=(tokens,) * 4 + (gauges,) * 2 + (lists, counts, counts),
        out_specs=(tokens,) * 3 + (gauges,) * 2,
        check_vma=False,
    )
```
